128 devices in a mesh: replica: 16 (over z_hi, x, core), shard: 8 (over z_lo, y).
Axes of the slice: x: 4, y: 4, z: 4 (z_hi: 2, z_lo: 2; z = z_hi * 2 + z_lo), core: 2. Of those that a mesh axis runs over, the one named last changes fastest.
Arguments:
- gate_pre: bfloat16 [16384, 3584], P(('replica', 'shard')), may hold values from -6 to 6
- up_pre: bfloat16 [16384, 3584], P(('replica', 'shard')), may hold values from -6 to 6
- out_grad: bfloat16 [16384, 8192], P(('replica', 'shard')), may hold values from -24 to 24
- w_down: bfloat16 [8192, 3584], P(None, 'shard'), may hold values from -0.0625 to 0.0625
- m_down: float32 [8192, 3584], P('replica', 'shard'), may hold values from -3 to 3
- v_down: float32 [8192, 3584], P('replica', 'shard'), may hold values from 0.02 to 0.5
Outputs:
- d_gate_up: bfloat16 [16384, 2, 3584], P(('replica', 'shard'))
- direction_down: bfloat16 [8192, 3584], P(None, 'shard')
- first_down: float32 [8192, 3584], P('replica', 'shard')
- second_down: float32 [8192, 3584], P('replica', 'shard')
The draws below stay inside these ranges and needn't reach their ends.
All inputs are finite; a program needn't handle non-finite values.
Results may differ from the reference program's by a relative error of at most 0.005.
Values may be sent and summed in bfloat16 or wider, within the bound.
A program may use at most 128 MiB of HBM per device.

```python
import math
import jax
import jax.numpy as jnp
from jax import lax

D = 8192
HID = 3584
TOKENS = 16384


def strengthened(drawn, stream_key, source, target, blocks, factor):
    def block_of(axis_at):
        return (jnp.arange(drawn.shape[axis_at]) // (drawn.shape[axis_at] // blocks)).reshape((-1,) + (1,) * (drawn.ndim - 1 - axis_at))

    one_side = jax.random.permutation(stream_key, blocks)[block_of(target)]
    other_side = (block_of(target) + blocks // 2) % blocks
    return jnp.where((block_of(source) == one_side) | (block_of(source) == other_side), factor * drawn, drawn)


def steps_of(own_key, dims, shards, least, high):
    def one(position, blocks):
        draws = jax.random.uniform(jax.random.fold_in(jax.random.fold_in(own_key, 6), position), (blocks,), jnp.float32, least / len(shards), high / len(shards))
        return jnp.repeat(jnp.exp(draws), dims[position] // blocks).reshape((-1,) + (1,) * (len(dims) - position - 1))

    gain = one(*shards[0])
    for cut in shards[1:]:
        gain = gain * one(*cut)
    return gain


def centred(rng, dims, deviation, reach, split=(), held_as=jnp.bfloat16):
    factor_of = steps_of(rng, dims, split, -0.22, 0.18) if split else 1.0
    result = jax.random.normal(rng, dims, jnp.float32) * deviation * factor_of
    return jnp.minimum(jnp.maximum(result, -reach), reach).astype(held_as)


def bell_draw_with(rng, shape, width, bound, pieces, heavy, kind=jnp.bfloat16):
    array = width * jax.random.normal(rng, shape, jnp.float32)
    if pieces:
        array = array * steps_of(rng, shape, pieces, -0.22, 0.18)
    return jnp.clip(strengthened(array, jax.random.fold_in(rng, 3), *heavy), -bound, bound).astype(kind)


def setup_inputs(seed: int = 0) -> dict:
    streams_of = jax.random.split(jax.random.key(seed), 7)
    return {
        "gate_pre": centred(streams_of[0], (TOKENS, HID), 1.0, 6.0, ((0, 128),)),
        "up_pre": centred(streams_of[1], (TOKENS, HID), 1.0, 6.0, ((0, 128),)),
        "out_grad": bell_draw_with(streams_of[2], (TOKENS, D), 1.0, 24.0, ((0, 128),), (0, 1, 128, 5.5)),
        "w_down": centred(streams_of[3], (D, HID), D ** -0.5, 0.0625, ((1, 8),)),
        "m_down": centred(streams_of[4], (D, HID), 0.5, 3.0, ((0, 16), (1, 8)), jnp.float32),
        "v_down": jnp.clip(jnp.exp(math.log(0.5) - 3.218876 * jax.random.uniform(streams_of[5], (D, HID), jnp.float32) ** steps_of(streams_of[5], (D, HID), ((0, 16), (1, 8)), -0.2, 0.2)), 0.02, 0.5),
    }


beta_one = 0.9
beta_two = 0.95
epsilon = 1e-08
bias_one = 1.0 - beta_one ** 10
bias_two = 1.0 - beta_two ** 10

def local_grads(gate, up, d_hidden):
    sig = jax.nn.sigmoid(gate)
    active = gate * sig
    hidden = (active * up).astype(jnp.bfloat16)
    d_gate = d_hidden * up * sig * (1.0 + gate * (1.0 - sig))
    d_up = d_hidden * active
    return (hidden, jnp.stack([d_gate, d_up], axis=1).astype(jnp.bfloat16))

def contract_rows(left, right):
    return lax.dot_general(left, right, (((0,), (0,)), ((), ())), preferred_element_type=jnp.float32)

def adam_step(first, second, grad):
    first_new = beta_one * first + (1.0 - beta_one) * grad
    second_new = beta_two * second + (1.0 - beta_two) * grad * grad
    direction = first_new / bias_one / (jnp.sqrt(second_new / bias_two) + epsilon)
    return (direction.astype(jnp.bfloat16), first_new, second_new)

def reference(gate_pre, up_pre, out_grad, w_down, m_down, v_down):
    gate = gate_pre.astype(jnp.float32)
    up = up_pre.astype(jnp.float32)
    d_hidden = jnp.dot(out_grad, w_down, preferred_element_type=jnp.float32)
    hidden, d_gate_up = local_grads(gate, up, d_hidden)
    factor = 1.0 / math.sqrt(TOKENS)
    grad_down = contract_rows(out_grad, hidden) * factor
    direction_down, first_down, second_down = adam_step(m_down, v_down, grad_down)
    return (d_gate_up, direction_down, first_down, second_down)
```

```python
import math

import jax
import jax.numpy as jnp
from jax import lax
from jax.experimental import pallas as pl
from jax.experimental.pallas import tpu as pltpu
from jax.sharding import PartitionSpec as P

beta_one = 0.9
beta_two = 0.95
epsilon = 1e-08
bias_one = 1.0 - beta_one**10
bias_two = 1.0 - beta_two**10

MESH = pl.DeviceIdType.MESH
BF = jnp.bfloat16
F32 = jnp.float32

TB = 128
HB = 448
ROWS = 512
TILE = 128
X_ORDER = (2, 1, 3, 0)
Y_ORDER = (2, 1, 3, 0)
STEPS = [(t, j) for t in range(2) for j in X_ORDER]


def kernel(
    gate, up, og, w, m, v,
    dgu, dirs, first, second,
    hid_own, hid, ogb, wbuf, rs_send, rs_recv, own, zs_send, zs_recv, gk, sw_send, sw_recv, dir_own,
    dk, cs_send, cs_recv, zd_send, zd_recv, yd_send, yd_recv,
    s1_s, s1_r, s2_s, s2_r, fw_s, fw_r, h1_s, h1_r, h2_s, h2_r, h3_s, h3_r, w_s, w_r, w_l,
    rs_s, rs_r, zs_s, zs_r, sw_s, sw_r, a_l, a_s, a_r, b_s, b_r, c_s, c_r,
    cs_s, cs_r, zd_s, zd_r, yd_s, yd_r,
):
    rep, sh = lax.axis_index("replica"), lax.axis_index("shard")
    zh, x, c = rep // 8, (rep // 2) % 4, rep % 2
    zl, y = sh // 4, sh % 4
    q = zl * 2 + c
    factor = 1.0 / math.sqrt(TB * 128)
    sends = []

    def dev(dzh=0, dx=0, dc=0, dzl=0, dy=0):
        return {
            "replica": ((zh + dzh) % 2) * 8 + ((x + dx) % 4) * 2 + (c + dc) % 2,
            "shard": ((zl + dzl) % 2) * 4 + (y + dy) % 4,
        }

    def push(src, dst, ssem, rsem, to, keep=True):
        cp = pltpu.make_async_remote_copy(
            src_ref=src, dst_ref=dst, send_sem=ssem, recv_sem=rsem, device_id=to, device_id_type=MESH
        )
        cp.start()
        if keep:
            sends.append((src, ssem))

    def landed(ref, sem):
        pltpu.make_async_copy(ref, ref, sem).wait()

    for i in range(28):
        cols = pl.ds(i * 128, 128)
        g = gate[:, cols].astype(F32)
        u = up[:, cols].astype(F32)
        hid_own[cols, :] = (g * jax.nn.sigmoid(g) * u).T.astype(BF)

    peers = [dev(dc=1), dev(dzl=1), dev(dzl=1, dc=1), dev(dzh=1), dev(dzh=1, dzl=1)]
    peers += [dev(dy=d) for d in (1, 2, 3)] + [dev(dx=d) for d in (1, 2, 3)]
    barrier = pltpu.get_barrier_semaphore()
    for peer in peers:
        pl.semaphore_signal(barrier, inc=1, device_id=peer, device_id_type=MESH)
    pl.semaphore_wait(barrier, len(peers))

    def tok(yy, qq):
        return pl.ds(pl.multiple_of((yy * 4 + qq) * TB, TB), TB)

    for n, dy in enumerate((2, 1, 3)):
        yd = (y + dy) % 4
        for b in range(2):
            rows = pl.ds(pl.multiple_of((b * 4 + yd) * HB, 16), HB)
            push(hid_own.at[rows, :], hid.at[b, :, tok(y, q)], h1_s.at[n, b], h1_r.at[n, b], dev(dy=dy))
    for b in range(2):
        rows = pl.ds(pl.multiple_of((b * 4 + y) * HB, 16), HB)
        pltpu.make_async_copy(hid_own.at[rows, :], hid.at[b, :, tok(y, q)], h1_r.at[3, b]).start()

    def d_row(zh2, dx, c2, zl2, t):
        r = zh2 * 8 + ((x + dx) % 4) * 2 + c2
        return pl.multiple_of(r * ROWS + zl2 * 256 + t * TILE, TILE)

    for k, (t, j) in enumerate(STEPS):
        for dzl, dc in ((1, 0), (1, 1), (0, 1), (0, 0)):
            for z in range(2):
                cols = pl.ds(d_row(z, j, (c + dc) % 2, (zl + dzl) % 2, t), TILE)
                dst = ogb.at[k, tok(y, q), pl.ds(z * TILE, TILE)]
                if dzl or dc:
                    push(og.at[:, cols], dst, s1_s.at[k], s1_r.at[k, q], dev(dc=dc, dzl=dzl), keep=False)
                else:
                    pltpu.make_async_copy(og.at[:, cols], dst, s1_r.at[k, q]).start()

    def slot(yy, lo=0, n=512):
        return pl.ds(pl.multiple_of(yy * 512 + lo, 128), n)

    def spread(k):
        for qq in range(4):
            landed(ogb.at[k, tok(y, qq), :], s1_r.at[k, qq])
        for n, dy in enumerate((1, 3)):
            push(ogb.at[k, slot(y), :], ogb.at[k, slot(y), :], s2_s.at[k, n], s2_r.at[k, n], dev(dy=dy))

    for k in range(2):
        spread(k)

    for n in range(4):
        ys = (y - (2, 1, 3, 0)[n]) % 4
        for b in range(2):
            landed(hid.at[b, :, tok(ys, q)], h1_r.at[n, b])
        blk = hid.at[:, :, tok(ys, q)]
        push(blk, blk, h2_s.at[n, 0], h2_r.at[n, 0], dev(dzl=1))
        push(blk, blk, h2_s.at[n, 1], h2_r.at[n, 1], dev(dc=1))

    for k in range(2, 8):
        spread(k)

    for n in range(4):
        ys = (y - (2, 1, 3, 0)[n]) % 4
        blk = hid.at[:, :, tok(ys, (1 - zl) * 2 + c)]
        landed(blk, h2_r.at[n, 0])
        push(blk, blk, h3_s.at[n], h3_r.at[n], dev(dc=1))
        landed(hid.at[:, :, tok(ys, zl * 2 + 1 - c)], h2_r.at[n, 1])

    for k, (t, j) in enumerate(STEPS):
        for z in range(2):
            half = pl.ds(z * TILE, TILE)
            mine = pl.ds(d_row(z, j, c, zl, t), TILE)
            theirs = pl.ds(d_row(z, j, c, 1 - zl, t), TILE)
            pltpu.make_async_copy(w.at[mine, :], wbuf.at[k, zl, half, :], w_l).start()
            push(w.at[theirs, :], wbuf.at[k, zl, half, :], w_s.at[t], w_r.at[t], dev(dzl=1, dzh=t), keep=False)

    for n in range(4):
        ys = (y - (2, 1, 3, 0)[n]) % 4
        landed(hid.at[:, :, tok(ys, (1 - zl) * 2 + 1 - c)], h3_r.at[n])

    def forward(k):
        down, upw = (y + 3) % 4, (y + 1) % 4
        landed(ogb.at[k, slot(down), :], s2_r.at[k, 0])
        part = ogb.at[k, slot(down, 0, 256), :]
        push(part, part, fw_s.at[k, 0], fw_r.at[k, 0], dev(dy=1))
        landed(ogb.at[k, slot(upw), :], s2_r.at[k, 1])
        part = ogb.at[k, slot(upw, 256, 256), :]
        push(part, part, fw_s.at[k, 1], fw_r.at[k, 1], dev(dy=3))

    def grad(k):
        t, j = STEPS[k]
        far = (y + 2) % 4
        landed(ogb.at[k, slot(far, 0, 256), :], fw_r.at[k, 0])
        landed(ogb.at[k, slot(far, 256, 256), :], fw_r.at[k, 1])

        @pl.loop(0, 2)
        def _(b):
            prod = jnp.dot(hid[b], ogb[k], preferred_element_type=F32)
            for z in range(2):
                part = prod[:, z * TILE : (z + 1) * TILE]
                if j:
                    rs_send[t, j - 1, z, b] = part.astype(BF)
                else:
                    own[t, z, b] = part

        if j:
            push(rs_send.at[t, j - 1], rs_recv.at[t, j - 1], rs_s.at[t, j - 1], rs_r.at[t, j - 1], dev(dx=j))

    def x_sum(t):
        for j in (1, 2, 3):
            landed(rs_recv.at[t, j - 1], rs_r.at[t, j - 1])

        @pl.loop(0, 2)
        def _(b):
            for z, mine in ((zh, True), (1 - zh, False)):
                total = own[t, z, b]
                for j in range(3):
                    total += rs_recv[t, j, z, b].astype(F32)
                if mine:
                    own[t, z, b] = total
                else:
                    zs_send[t, b] = total.astype(BF)

        push(zs_send.at[t], zs_recv.at[t], zs_s.at[t], zs_r.at[t], dev(dzh=1))

    def z_sum(t):
        landed(zs_recv.at[t], zs_r.at[t])
        gk[t] = own[t, zh, zl] + zs_recv[t, zl].astype(F32)
        sw_send[t] = (own[t, zh, 1 - zl] + zs_recv[t, 1 - zl].astype(F32)).astype(BF)
        push(sw_send.at[t], sw_recv.at[t], sw_s.at[t], sw_r.at[t], dev(dzl=1))

    def adam(t):
        landed(sw_recv.at[t], sw_r.at[t])
        for half, g_units in ((zl, gk[t]), (1 - zl, sw_recv[t].astype(F32))):
            g = g_units.T * factor
            rows = pl.ds(pl.multiple_of(half * 256 + t * TILE, TILE), TILE)
            first_new = beta_one * m[rows, :] + (1.0 - beta_one) * g
            second_new = beta_two * v[rows, :] + (1.0 - beta_two) * g * g
            first[rows, :] = first_new
            second[rows, :] = second_new
            direction = first_new / bias_one / (jnp.sqrt(second_new / bias_two) + epsilon)
            dir_own[t, half] = direction.astype(BF)
        pltpu.make_async_copy(dir_own.at[t], dirs.at[c, t, x, zh], a_l.at[t]).start()
        push(dir_own.at[t], dirs.at[c, t, x, zh], a_s.at[t], a_r.at[t], dev(dzh=1))

    def dir_x(t):
        landed(dirs.at[c, t, x, zh], a_l.at[t])
        landed(dirs.at[c, t, x, 1 - zh], a_r.at[t])
        blk = dirs.at[c, t, x]
        for j in (2, 1, 3):
            push(blk, blk, b_s.at[t, j], b_r.at[t, j], dev(dx=j))
        push(blk, blk, c_s.at[t, 0], c_r.at[t, 0], dev(dc=1))

    def dir_core(t):
        for j in (1, 3, 2):
            blk = dirs.at[c, t, (x - j) % 4]
            landed(blk, b_r.at[t, j])
            push(blk, blk, c_s.at[t, j], c_r.at[t, j], dev(dc=1))

    def dir_end(t):
        for j in range(4):
            landed(dirs.at[1 - c, t, (x - j) % 4], c_r.at[t, j])

    def dh_dot(i):
        ys = (y + Y_ORDER[i]) % 4

        @pl.loop(0, 2)
        def _(b):
            total = None
            for k in range(8):
                part = jnp.dot(ogb[k, slot(ys), :], wbuf[k, b], preferred_element_type=F32)
                total = part if total is None else total + part
            ogs = total.reshape(2, 2, TB, HB)
            for zz in range(2):
                both = ogs[zz]
                dk[i, zz, b] = jnp.where(c == 0, both[0], both[1])
                cs_send[i, zz, b] = jnp.where(c == 0, both[1], both[0]).astype(BF)

        push(cs_send.at[i], cs_recv.at[i], cs_s.at[i], cs_r.at[i], dev(dc=1))

    def dh_core(i):
        landed(cs_recv.at[i], cs_r.at[i])

        @pl.loop(0, 2)
        def _(b):
            dk[i, zl, b] = dk[i, zl, b] + cs_recv[i, zl, b].astype(F32)
            zd_send[i, b] = (dk[i, 1 - zl, b] + cs_recv[i, 1 - zl, b].astype(F32)).astype(BF)

        push(zd_send.at[i], zd_recv.at[i], zd_s.at[i], zd_r.at[i], dev(dzl=1))

    def dh_z(i):
        landed(zd_recv.at[i], zd_r.at[i])
        dy = Y_ORDER[i]
        for b in range(2):
            total = (dk[i, zl, b] + zd_recv[i, b].astype(F32)).astype(BF)
            if dy:
                yd_send[i, b] = total
            else:
                yd_recv[y, b] = total
        if dy:
            push(yd_send.at[i], yd_recv.at[y], yd_s.at[i], yd_r.at[i], dev(dy=dy))

    forward(0)
    for k in range(8):
        if k < 7:
            forward(k + 1)
        grad(k)
        if k == 5:
            x_sum(0)
        if k == 6:
            z_sum(0)
        if k == 7:
            adam(0)
    x_sum(1)
    landed(wbuf.at[:, zl], w_l)
    for t in range(2):
        landed(wbuf.at[pl.ds(t * 4, 4), 1 - zl], w_r.at[t])
    dh_dot(0)
    z_sum(1)
    dir_x(0)
    dh_dot(1)
    dh_core(0)
    adam(1)
    dh_dot(2)
    dh_core(1)
    dh_z(0)
    dir_x(1)
    dh_dot(3)
    dh_core(2)
    dh_z(1)
    dir_core(0)
    dh_core(3)
    dh_z(2)
    dh_z(3)
    for i in range(3):
        ys = (y - Y_ORDER[i]) % 4
        landed(yd_recv.at[ys], yd_r.at[i])
    for b in range(2):
        for ys in range(4):
            cols = pl.ds((b * 4 + ys) * HB, HB)
            d = yd_recv[ys, b].astype(F32)
            g = gate[:, cols].astype(F32)
            u = up[:, cols].astype(F32)
            sig = jax.nn.sigmoid(g)
            dgu[0, :, cols] = (d * u * sig * (1.0 + g * (1.0 - sig))).astype(BF)
            dgu[1, :, cols] = (d * (g * sig)).astype(BF)
    dir_core(1)
    dir_end(0)
    dir_end(1)

    for src, sem in sends:
        landed(src, sem)
    for k in range(8):
        landed(ogb.at[k, pl.ds(0, 384), :], s1_s.at[k])
    for t in range(2):
        landed(wbuf.at[pl.ds(t * 4, 4), 0], w_s.at[t])


def local(gate_pre, up_pre, out_grad, w_down, m_down, v_down):
    vmem = pl.BlockSpec(memory_space=pltpu.VMEM)
    hbm = pl.BlockSpec(memory_space=pl.ANY)
    dma = pltpu.SemaphoreType.DMA
    scratch = [
        pltpu.VMEM((8 * HB, TB), BF),
        pltpu.VMEM((2, HB, 16 * TB), BF),
        pltpu.VMEM((8, 2048, 256), BF),
        pltpu.VMEM((8, 2, 256, HB), BF),
        pltpu.VMEM((2, 3, 2, 2, HB, TILE), BF),
        pltpu.VMEM((2, 3, 2, 2, HB, TILE), BF),
        pltpu.VMEM((2, 2, 2, HB, TILE), F32),
        pltpu.VMEM((2, 2, HB, TILE), BF),
        pltpu.VMEM((2, 2, HB, TILE), BF),
        pltpu.VMEM((2, HB, TILE), F32),
        pltpu.VMEM((2, HB, TILE), BF),
        pltpu.VMEM((2, HB, TILE), BF),
        pltpu.VMEM((2, 2, TILE, HB), BF),
        pltpu.VMEM((4, 2, 2, TB, HB), F32),
        pltpu.VMEM((4, 2, 2, TB, HB), BF),
        pltpu.VMEM((4, 2, 2, TB, HB), BF),
        pltpu.VMEM((4, 2, TB, HB), BF),
        pltpu.VMEM((4, 2, TB, HB), BF),
        pltpu.VMEM((3, 2, TB, HB), BF),
        pltpu.VMEM((4, 2, TB, HB), BF),
        dma((8,)), dma((8, 4)),
        dma((8, 2)), dma((8, 2)),
        dma((8, 2)), dma((8, 2)),
        dma((3, 2)), dma((4, 2)),
        dma((4, 2)), dma((4, 2)),
        dma((4,)), dma((4,)),
        dma((2,)), dma((2,)), dma,
        dma((2, 3)), dma((2, 3)),
        dma((2,)), dma((2,)),
        dma((2,)), dma((2,)),
        dma((2,)), dma((2,)), dma((2,)),
        dma((2, 4)), dma((2, 4)),
        dma((2, 4)), dma((2, 4)),
        dma((4,)), dma((4,)),
        dma((4,)), dma((4,)),
        dma((3,)), dma((3,)),
    ]
    dgu, dirs, first, second = pl.pallas_call(
        kernel,
        name="step",
        out_shape=(
            jax.ShapeDtypeStruct((2, TB, 8 * HB), BF),
            jax.ShapeDtypeStruct((2, 2, 4, 2, 2, TILE, HB), BF),
            jax.ShapeDtypeStruct((ROWS, HB), F32),
            jax.ShapeDtypeStruct((ROWS, HB), F32),
        ),
        in_specs=[vmem, vmem, vmem, hbm, vmem, vmem],
        out_specs=(vmem, hbm, vmem, vmem),
        scratch_shapes=scratch,
        compiler_params=pltpu.CompilerParams(
            collective_id=0, has_side_effects=True, vmem_limit_bytes=60 << 20
        ),
        cost_estimate=pl.CostEstimate(flops=15 * 10**9, bytes_accessed=40 * 10**6, transcendentals=0),
    )(gate_pre, up_pre, out_grad, w_down, m_down, v_down)
    direction = dirs.transpose(3, 2, 0, 4, 1, 5, 6).reshape(16 * ROWS, HB)
    return (dgu.transpose(1, 0, 2), direction, first, second)


def solution(mesh):
    return jax.shard_map(
        local,
        mesh=mesh,
        in_specs=(
            P(("replica", "shard"), None),
            P(("replica", "shard"), None),
            P(("replica", "shard"), None),
            P(None, "shard"),
            P("replica", "shard"),
            P("replica", "shard"),
        ),
        out_specs=(
            P(("replica", "shard"), None, None),
            P(None, "shard"),
            P("replica", "shard"),
            P("replica", "shard"),
        ),
        check_vma=False,
    )
```

```python
import math

import jax
import jax.numpy as jnp
from jax import lax
from jax.experimental import pallas as pl
from jax.experimental.pallas import tpu as pltpu
from jax.sharding import PartitionSpec as P

beta_one = 0.9
beta_two = 0.95
epsilon = 1e-08
bias_one = 1.0 - beta_one**10
bias_two = 1.0 - beta_two**10

MESH = pl.DeviceIdType.MESH
BF = jnp.bfloat16
F32 = jnp.float32

TB = 128
HB = 448
ROWS = 512
TILE = 128
X_ORDER = (2, 1, 3, 0)
Y_ORDER = (2, 1, 3, 0)
STEPS = [(t, j) for t in range(2) for j in X_ORDER]


def kernel(
    gate, up, og, w, m, v,
    dgu, dirs, first, second,
    hid_own, d_own, hid, ogb, wbuf, rs_send, rs_recv, own, zs_send, zs_recv, gk, dir_own,
    dk, cs_send, cs_recv, zd_send, zd_recv, yd_send, yd_recv,
    s1_s, s1_r, s2_s, s2_r, fw_s, fw_r, h1_s, h1_r, h2_s, h2_r, h3_s, h3_r, w_s, w_r, w_l,
    rs_s, rs_r, zs_s, zs_r, a_l, a_s, a_r, b_s, b_r, c_s, c_r,
    cs_s, cs_r, zd_s, zd_r, yd_s, yd_r,
):
    rep, sh = lax.axis_index("replica"), lax.axis_index("shard")
    zh, x, c = rep // 8, (rep // 2) % 4, rep % 2
    zl, y = sh // 4, sh % 4
    q = zl * 2 + c
    factor = 1.0 / math.sqrt(TB * 128)
    sends = []

    def dev(dzh=0, dx=0, dc=0, dzl=0, dy=0):
        return {
            "replica": ((zh + dzh) % 2) * 8 + ((x + dx) % 4) * 2 + (c + dc) % 2,
            "shard": ((zl + dzl) % 2) * 4 + (y + dy) % 4,
        }

    def push(src, dst, ssem, rsem, to, keep=True):
        cp = pltpu.make_async_remote_copy(
            src_ref=src, dst_ref=dst, send_sem=ssem, recv_sem=rsem, device_id=to, device_id_type=MESH
        )
        cp.start()
        if keep:
            sends.append((src, ssem))

    def landed(ref, sem):
        pltpu.make_async_copy(ref, ref, sem).wait()

    for i in range(28):
        cols = pl.ds(i * 128, 128)
        g = gate[:, cols].astype(F32)
        u = up[:, cols].astype(F32)
        hid_own[cols, :] = (g * jax.nn.sigmoid(g) * u).T.astype(BF)

    peers = [dev(dc=1), dev(dzl=1), dev(dzl=1, dc=1), dev(dzh=1), dev(dzh=1, dzl=1)]
    peers += [dev(dy=d) for d in (1, 2, 3)] + [dev(dx=d) for d in (1, 2, 3)]
    barrier = pltpu.get_barrier_semaphore()
    for peer in peers:
        pl.semaphore_signal(barrier, inc=1, device_id=peer, device_id_type=MESH)
    pl.semaphore_wait(barrier, len(peers))

    def tok(yy, qq):
        return pl.ds(pl.multiple_of((yy * 4 + qq) * TB, TB), TB)

    def d_row(zh2, dx, c2, zl2, t):
        r = zh2 * 8 + ((x + dx) % 4) * 2 + c2
        return pl.multiple_of(r * ROWS + t * 256 + zl2 * TILE, TILE)

    def slot(yy, lo=0, n=512):
        return pl.ds(pl.multiple_of(yy * 512 + lo, 128), n)

    H_ORDER = (0, 1, 3, 2)

    def hid_y(n):
        dy = H_ORDER[n]
        for b in range(2):
            rows = pl.ds(pl.multiple_of((b * 4 + (y + dy) % 4) * HB, 16), HB)
            src, dst = hid_own.at[rows, :], hid.at[b, :, tok(y, q)]
            if dy:
                push(src, dst, h1_s.at[n, b], h1_r.at[n, b], dev(dy=dy))
            else:
                pltpu.make_async_copy(src, dst, h1_r.at[n, b]).start()

    def hid_z(n):
        ys = (y - H_ORDER[n]) % 4
        for b in range(2):
            landed(hid.at[b, :, tok(ys, q)], h1_r.at[n, b])
        blk = hid.at[:, :, tok(ys, q)]
        push(blk, blk, h2_s.at[n, 0], h2_r.at[n, 0], dev(dzl=1))
        push(blk, blk, h2_s.at[n, 1], h2_r.at[n, 1], dev(dc=1))

    def hid_core(n):
        ys = (y - H_ORDER[n]) % 4
        blk = hid.at[:, :, tok(ys, (1 - zl) * 2 + c)]
        landed(blk, h2_r.at[n, 0])
        push(blk, blk, h3_s.at[n], h3_r.at[n], dev(dc=1))

    def hid_end(n):
        ys = (y - H_ORDER[n]) % 4
        landed(hid.at[:, :, tok(ys, zl * 2 + 1 - c)], h2_r.at[n, 1])
        landed(hid.at[:, :, tok(ys, (1 - zl) * 2 + 1 - c)], h3_r.at[n])

    def quarter(k):
        t, j = STEPS[k]
        for dzl, dc in ((1, 0), (1, 1), (0, 1), (0, 0)):
            for z in range(2):
                cols = pl.ds(d_row(z, j, (c + dc) % 2, (zl + dzl) % 2, t), TILE)
                dst = ogb.at[k, tok(y, q), pl.ds(z * TILE, TILE)]
                if dzl or dc:
                    push(og.at[:, cols], dst, s1_s.at[k], s1_r.at[k, q], dev(dc=dc, dzl=dzl), keep=False)
                else:
                    pltpu.make_async_copy(og.at[:, cols], dst, s1_r.at[k, q]).start()

    def spread(k):
        for qq in range(4):
            landed(ogb.at[k, tok(y, qq), :], s1_r.at[k, qq])
        for n, dy in enumerate((1, 3)):
            push(ogb.at[k, slot(y), :], ogb.at[k, slot(y), :], s2_s.at[k, n], s2_r.at[k, n], dev(dy=dy))

    def weights():
        for k, (t, j) in enumerate(STEPS):
            for z in range(2):
                half = pl.ds(z * TILE, TILE)
                mine = pl.ds(d_row(z, j, c, zl, t), TILE)
                theirs = pl.ds(d_row(z, j, c, 1 - zl, t), TILE)
                pltpu.make_async_copy(w.at[:, mine], wbuf.at[k, zl, :, half], w_l).start()
                push(w.at[:, theirs], wbuf.at[k, zl, :, half], w_s.at[t], w_r.at[t], dev(dzl=1, dzh=t), keep=False)

    def forward(k):
        down, upw = (y + 3) % 4, (y + 1) % 4
        landed(ogb.at[k, slot(down), :], s2_r.at[k, 0])
        part = ogb.at[k, slot(down, 0, 256), :]
        push(part, part, fw_s.at[k, 0], fw_r.at[k, 0], dev(dy=1))
        landed(ogb.at[k, slot(upw), :], s2_r.at[k, 1])
        part = ogb.at[k, slot(upw, 256, 256), :]
        push(part, part, fw_s.at[k, 1], fw_r.at[k, 1], dev(dy=3))

    def grad(k):
        t, j = STEPS[k]
        far = (y + 2) % 4
        landed(ogb.at[k, slot(far, 0, 256), :], fw_r.at[k, 0])
        landed(ogb.at[k, slot(far, 256, 256), :], fw_r.at[k, 1])

        @pl.loop(0, 2)
        def _(b):
            prod = jnp.dot(hid[b], ogb[k], preferred_element_type=F32)
            for z in range(2):
                part = prod[:, z * TILE : (z + 1) * TILE]
                if j:
                    rs_send[t, j - 1, z, b] = part.astype(BF)
                else:
                    own[t, z, b] = part

        if j:
            push(rs_send.at[t, j - 1], rs_recv.at[t, j - 1], rs_s.at[t, j - 1], rs_r.at[t, j - 1], dev(dx=j))

    def x_sum(t):
        for j in (1, 2, 3):
            landed(rs_recv.at[t, j - 1], rs_r.at[t, j - 1])

        def total(z, b):
            out = own[t, z, b]
            for j in range(3):
                out += rs_recv[t, j, z, b].astype(F32)
            return out

        for n, (z, b) in enumerate(((1 - zh, zl), (zh, 1 - zl), (1 - zh, 1 - zl))):
            zs_send[t, n] = total(z, b).astype(BF)
            to = (dev(dzh=1), dev(dzl=1), dev(dzh=1, dzl=1))[n]
            push(zs_send.at[t, n], zs_recv.at[t, n], zs_s.at[t, n], zs_r.at[t, n], to)
        gk[t] = total(zh, zl)

    def block(zh2, x2, c2, t):
        r = zh2 * 8 + x2 * 2 + c2
        return dirs.at[:, pl.ds(pl.multiple_of(r * ROWS + t * 256, 256), 256)]

    def adam(t):
        for n in range(3):
            landed(zs_recv.at[t, n], zs_r.at[t, n])
        mine = gk[t] + zs_recv[t, 0].astype(F32)
        others = zs_recv[t, 1].astype(F32) + zs_recv[t, 2].astype(F32)
        for half, g_sum in ((zl, mine), (1 - zl, others)):
            g = g_sum * factor
            cols = pl.ds(pl.multiple_of(t * 256 + half * TILE, TILE), TILE)
            first_new = beta_one * m[:, cols] + (1.0 - beta_one) * g
            second_new = beta_two * v[:, cols] + (1.0 - beta_two) * g * g
            first[:, cols] = first_new
            second[:, cols] = second_new
            direction = first_new / bias_one / (jnp.sqrt(second_new / bias_two) + epsilon)
            dir_own[t, :, pl.ds(pl.multiple_of(half * TILE, TILE), TILE)] = direction.astype(BF)
        place, src = block(zh, x, c, t), dir_own.at[t]
        push(src, place, a_s.at[t], a_r.at[t], dev(dzh=1))
        for j in (2, 1, 3):
            push(src, place, b_s.at[t, j, 0], b_r.at[t, j, 0], dev(dx=j))
        push(src, place, c_s.at[t, 0, 0], c_r.at[t, 0, 0], dev(dc=1))
        pltpu.make_async_copy(src, place, a_l.at[t]).start()

    def dir_x(t):
        blk = block(1 - zh, x, c, t)
        landed(blk, a_r.at[t])
        for j in (2, 1, 3):
            push(blk, blk, b_s.at[t, j, 1], b_r.at[t, j, 1], dev(dx=j))
        push(blk, blk, c_s.at[t, 0, 1], c_r.at[t, 0, 1], dev(dc=1))

    def dir_core(t, n):
        for j in (1, 3, 2):
            blk = block(zh if n == 0 else 1 - zh, (x - j) % 4, c, t)
            landed(blk, b_r.at[t, j, n])
            push(blk, blk, c_s.at[t, j, n], c_r.at[t, j, n], dev(dc=1))

    def dir_end(t):
        landed(block(zh, x, c, t), a_l.at[t])
        for j in range(4):
            for n in range(2):
                landed(block(zh if n == 0 else 1 - zh, (x - j) % 4, 1 - c, t), c_r.at[t, j, n])

    def dh_dots(i, b, ks):
        total = None
        for k in ks:
            part = lax.dot_general(
                wbuf[k, b], ogb[k, slot((y + Y_ORDER[i]) % 4), :],
                (((1,), (1,)), ((), ())), preferred_element_type=F32,
            )
            total = part if total is None else total + part
        return total

    def dh_early(i):
        @pl.loop(0, 2)
        def _(b):
            dk[i, b] = dh_dots(i, b, range(4))

    def lanes(zz):
        return pl.ds(pl.multiple_of(zz * TB, TB), TB)

    def dh_late(i):
        @pl.loop(0, 2)
        def _(b):
            total = dh_dots(i, b, range(4, 8)) + dk[i, b]
            for zz in range(2):
                lo = total[:, zz * 256 : zz * 256 + 128]
                hi = total[:, zz * 256 + 128 : zz * 256 + 256]
                dk[i, b, :, lanes(zz)] = jnp.where(c == 0, lo, hi)
                cs_send[i, zz, b] = jnp.where(c == 0, hi, lo).astype(BF)

        push(cs_send.at[i], cs_recv.at[i], cs_s.at[i], cs_r.at[i], dev(dc=1))

    def dh_core(i):
        landed(cs_recv.at[i], cs_r.at[i])

        @pl.loop(0, 2)
        def _(b):
            dk[i, b, :, lanes(zl)] = dk[i, b, :, lanes(zl)] + cs_recv[i, zl, b].astype(F32)
            zd_send[i, b] = (dk[i, b, :, lanes(1 - zl)] + cs_recv[i, 1 - zl, b].astype(F32)).astype(BF)

        push(zd_send.at[i], zd_recv.at[i], zd_s.at[i], zd_r.at[i], dev(dzl=1))

    def dh_z(i):
        landed(zd_recv.at[i], zd_r.at[i])
        dy = Y_ORDER[i]
        for b in range(2):
            total = (dk[i, b, :, lanes(zl)] + zd_recv[i, b].astype(F32)).astype(BF)
            if dy:
                yd_send[i, b] = total
            else:
                yd_recv[y, b] = total
        if dy:
            push(yd_send.at[i], yd_recv.at[y], yd_s.at[i], yd_r.at[i], dev(dy=dy))

    def cotangents():
        for i in range(3):
            ys = (y - Y_ORDER[i]) % 4
            landed(yd_recv.at[ys], yd_r.at[i])
        for b in range(2):
            for ys in range(4):
                d_own[pl.ds((b * 4 + ys) * HB, HB), :] = yd_recv[ys, b]
        for i in range(28):
            cols = pl.ds(i * 128, 128)
            d = d_own[cols, :].astype(F32).T
            g = gate[:, cols].astype(F32)
            u = up[:, cols].astype(F32)
            sig = jax.nn.sigmoid(g)
            dgu[0, :, cols] = (d * u * sig * (1.0 + g * (1.0 - sig))).astype(BF)
            dgu[1, :, cols] = (d * (g * sig)).astype(BF)

    for n in range(1, 4):
        hid_y(n)
    hid_y(0)
    quarter(0)
    hid_z(0)
    quarter(1)
    quarter(2)
    spread(0)
    spread(1)
    hid_z(1)
    quarter(3)
    hid_z(2)
    quarter(4)
    hid_core(0)
    hid_z(3)
    for k in (5, 6, 7):
        quarter(k)
    forward(0)
    spread(2)
    hid_core(1)
    forward(1)
    spread(3)
    hid_core(2)
    forward(2)
    spread(4)
    hid_core(3)
    weights()
    for n in range(4):
        hid_end(n)
    grad(0)
    grad(1)
    forward(3)
    spread(5)
    grad(2)
    forward(4)
    spread(6)
    grad(3)
    landed(wbuf.at[:, zl], w_l)
    landed(wbuf.at[pl.ds(0, 4), 1 - zl], w_r.at[0])
    dh_early(0)
    forward(5)
    spread(7)
    grad(4)
    x_sum(0)
    dh_early(1)
    forward(6)
    grad(5)
    adam(0)
    dh_early(2)
    forward(7)
    grad(6)
    dir_x(0)
    dh_early(3)
    grad(7)
    landed(wbuf.at[pl.ds(4, 4), 1 - zl], w_r.at[1])
    dh_late(0)
    x_sum(1)
    dh_late(1)
    dh_core(0)
    dh_late(2)
    dh_core(1)
    adam(1)
    dh_late(3)
    dh_z(0)
    dh_core(2)
    dir_x(1)
    dir_core(0, 0)
    dir_core(0, 1)
    dh_z(1)
    dh_core(3)
    dh_z(2)
    dh_z(3)
    dir_core(1, 0)
    cotangents()
    dir_core(1, 1)
    dir_end(0)
    dir_end(1)

    for src, sem in sends:
        landed(src, sem)
    for k in range(8):
        landed(ogb.at[k, pl.ds(0, 384), :], s1_s.at[k])
    for t in range(2):
        landed(wbuf.at[pl.ds(t * 4, 4), 0], w_s.at[t])


def local(gate_pre, up_pre, out_grad, w_down, m_down, v_down):
    vmem = pl.BlockSpec(memory_space=pltpu.VMEM)
    hbm = pl.BlockSpec(memory_space=pl.ANY)
    dma = pltpu.SemaphoreType.DMA
    scratch = [
        pltpu.VMEM((8 * HB, TB), BF),
        pltpu.VMEM((8 * HB, TB), BF),
        pltpu.VMEM((2, HB, 16 * TB), BF),
        pltpu.VMEM((8, 2048, 256), BF),
        pltpu.VMEM((8, 2, HB, 256), BF),
        pltpu.VMEM((2, 3, 2, 2, HB, TILE), BF),
        pltpu.VMEM((2, 3, 2, 2, HB, TILE), BF),
        pltpu.VMEM((2, 2, 2, HB, TILE), F32),
        pltpu.VMEM((2, 3, HB, TILE), BF),
        pltpu.VMEM((2, 3, HB, TILE), BF),
        pltpu.VMEM((2, HB, TILE), F32),
        pltpu.VMEM((2, HB, 256), BF),
        pltpu.VMEM((4, 2, HB, 512), F32),
        pltpu.VMEM((4, 2, 2, HB, TB), BF),
        pltpu.VMEM((4, 2, 2, HB, TB), BF),
        pltpu.VMEM((4, 2, HB, TB), BF),
        pltpu.VMEM((4, 2, HB, TB), BF),
        pltpu.VMEM((3, 2, HB, TB), BF),
        pltpu.VMEM((4, 2, HB, TB), BF),
        dma((8,)), dma((8, 4)),
        dma((8, 2)), dma((8, 2)),
        dma((8, 2)), dma((8, 2)),
        dma((4, 2)), dma((4, 2)),
        dma((4, 2)), dma((4, 2)),
        dma((4,)), dma((4,)),
        dma((2,)), dma((2,)), dma,
        dma((2, 3)), dma((2, 3)),
        dma((2, 3)), dma((2, 3)),
        dma((2,)), dma((2,)), dma((2,)),
        dma((2, 4, 2)), dma((2, 4, 2)),
        dma((2, 4, 2)), dma((2, 4, 2)),
        dma((4,)), dma((4,)),
        dma((4,)), dma((4,)),
        dma((3,)), dma((3,)),
    ]
    dgu, dirs, first, second = pl.pallas_call(
        kernel,
        name="step",
        out_shape=(
            jax.ShapeDtypeStruct((2, TB, 8 * HB), BF),
            jax.ShapeDtypeStruct((HB, 16 * ROWS), BF),
            jax.ShapeDtypeStruct((HB, ROWS), F32),
            jax.ShapeDtypeStruct((HB, ROWS), F32),
        ),
        in_specs=[vmem, vmem, vmem, hbm, vmem, vmem],
        out_specs=(vmem, hbm, vmem, vmem),
        scratch_shapes=scratch,
        compiler_params=pltpu.CompilerParams(
            collective_id=0, has_side_effects=True, vmem_limit_bytes=60 << 20
        ),
        cost_estimate=pl.CostEstimate(flops=15 * 10**9, bytes_accessed=40 * 10**6, transcendentals=0),
    )(gate_pre, up_pre, out_grad, w_down.T, m_down.T, v_down.T)
    return (dgu.transpose(1, 0, 2), dirs.T, first.T, second.T)


def solution(mesh):
    return jax.shard_map(
        local,
        mesh=mesh,
        in_specs=(
            P(("replica", "shard"), None),
            P(("replica", "shard"), None),
            P(("replica", "shard"), None),
            P(None, "shard"),
            P("replica", "shard"),
            P("replica", "shard"),
        ),
        out_specs=(
            P(("replica", "shard"), None, None),
            P(None, "shard"),
            P("replica", "shard"),
            P("replica", "shard"),
        ),
        check_vma=False,
    )
```

```python
import math

import jax
import jax.numpy as jnp
from jax import lax
from jax.experimental import pallas as pl
from jax.experimental.pallas import tpu as pltpu
from jax.sharding import PartitionSpec as P

beta_one = 0.9
beta_two = 0.95
epsilon = 1e-08
bias_one = 1.0 - beta_one**10
bias_two = 1.0 - beta_two**10

MESH = pl.DeviceIdType.MESH
BF = jnp.bfloat16
F32 = jnp.float32

TB = 128
HB = 448
ROWS = 512
TILE = 128
X_ORDER = (2, 1, 3, 0)
Y_ORDER = (2, 1, 3, 0)
STEPS = [(t, j) for t in range(2) for j in X_ORDER]


def kernel(
    gate, up, og, w, m, v,
    dgu, dirs, first, second,
    hid_own, d_own, hid, ogb, wbuf, rs_send, rs_recv, own, zs_send, zs_recv, gk, dir_own,
    dk, cs_send, cs_recv, zd_send, zd_recv, yd_send, yd_recv,
    s1_s, s1_r, s2_s, s2_r, fw_s, fw_r, h1_s, h1_r, h2_s, h2_r, h3_s, h3_r, w_s, w_r, w_l,
    rs_s, rs_r, zs_s, zs_r, a_l, a_s, a_r, b_s, b_r, f_s, f_r, c_s, c_r,
    cs_s, cs_r, zd_s, zd_r, yd_s, yd_r,
):
    rep, sh = lax.axis_index("replica"), lax.axis_index("shard")
    zh, x, c = rep // 8, (rep // 2) % 4, rep % 2
    zl, y = sh // 4, sh % 4
    q = zl * 2 + c
    factor = 1.0 / math.sqrt(TB * 128)
    sends = []

    def dev(dzh=0, dx=0, dc=0, dzl=0, dy=0):
        return {
            "replica": ((zh + dzh) % 2) * 8 + ((x + dx) % 4) * 2 + (c + dc) % 2,
            "shard": ((zl + dzl) % 2) * 4 + (y + dy) % 4,
        }

    def push(src, dst, ssem, rsem, to, keep=True):
        cp = pltpu.make_async_remote_copy(
            src_ref=src, dst_ref=dst, send_sem=ssem, recv_sem=rsem, device_id=to, device_id_type=MESH
        )
        cp.start()
        if keep:
            sends.append((src, ssem))

    def landed(ref, sem):
        pltpu.make_async_copy(ref, ref, sem).wait()

    for i in range(28):
        cols = pl.ds(i * 128, 128)
        g = gate[:, cols].astype(F32)
        u = up[:, cols].astype(F32)
        hid_own[cols, :] = (g * jax.nn.sigmoid(g) * u).T.astype(BF)

    peers = [dev(dc=1), dev(dzl=1), dev(dzl=1, dc=1), dev(dzh=1), dev(dzh=1, dzl=1)]
    peers += [dev(dy=d) for d in (1, 2, 3)] + [dev(dx=d) for d in (1, 2, 3)]
    barrier = pltpu.get_barrier_semaphore()
    for peer in peers:
        pl.semaphore_signal(barrier, inc=1, device_id=peer, device_id_type=MESH)
    pl.semaphore_wait(barrier, len(peers))

    def tok(yy, qq):
        return pl.ds(pl.multiple_of((yy * 4 + qq) * TB, TB), TB)

    def d_row(zh2, dx, c2, zl2, t):
        r = zh2 * 8 + ((x + dx) % 4) * 2 + c2
        return pl.multiple_of(r * ROWS + t * 256 + zl2 * TILE, TILE)

    def slot(yy, lo=0, n=512):
        return pl.ds(pl.multiple_of(yy * 512 + lo, 128), n)

    H_ORDER = (0, 1, 3, 2)

    def hid_y(n):
        dy = H_ORDER[n]
        for b in range(2):
            rows = pl.ds(pl.multiple_of((b * 4 + (y + dy) % 4) * HB, 16), HB)
            src, dst = hid_own.at[rows, :], hid.at[b, :, tok(y, q)]
            if dy:
                push(src, dst, h1_s.at[n, b], h1_r.at[n, b], dev(dy=dy))
            else:
                pltpu.make_async_copy(src, dst, h1_r.at[n, b]).start()

    def hid_z(n):
        ys = (y - H_ORDER[n]) % 4
        for b in range(2):
            landed(hid.at[b, :, tok(ys, q)], h1_r.at[n, b])
        blk = hid.at[:, :, tok(ys, q)]
        push(blk, blk, h2_s.at[n, 0], h2_r.at[n, 0], dev(dzl=1))
        push(blk, blk, h2_s.at[n, 1], h2_r.at[n, 1], dev(dc=1))

    def hid_core(n):
        ys = (y - H_ORDER[n]) % 4
        blk = hid.at[:, :, tok(ys, (1 - zl) * 2 + c)]
        landed(blk, h2_r.at[n, 0])
        push(blk, blk, h3_s.at[n], h3_r.at[n], dev(dc=1))

    def hid_end(n):
        ys = (y - H_ORDER[n]) % 4
        landed(hid.at[:, :, tok(ys, zl * 2 + 1 - c)], h2_r.at[n, 1])
        landed(hid.at[:, :, tok(ys, (1 - zl) * 2 + 1 - c)], h3_r.at[n])

    def quarter(k):
        t, j = STEPS[k]
        for dzl, dc in ((1, 0), (1, 1), (0, 1), (0, 0)):
            for z in range(2):
                cols = pl.ds(d_row(z, j, (c + dc) % 2, (zl + dzl) % 2, t), TILE)
                dst = ogb.at[k, tok(y, q), pl.ds(z * TILE, TILE)]
                if dzl or dc:
                    push(og.at[:, cols], dst, s1_s.at[k], s1_r.at[k, q], dev(dc=dc, dzl=dzl), keep=False)
                else:
                    pltpu.make_async_copy(og.at[:, cols], dst, s1_r.at[k, q]).start()

    def spread(k):
        for qq in range(4):
            landed(ogb.at[k, tok(y, qq), :], s1_r.at[k, qq])
        for n, dy in enumerate((1, 3)):
            push(ogb.at[k, slot(y), :], ogb.at[k, slot(y), :], s2_s.at[k, n], s2_r.at[k, n], dev(dy=dy))

    def weights():
        for k, (t, j) in enumerate(STEPS):
            for z in range(2):
                half = pl.ds(z * TILE, TILE)
                mine = pl.ds(d_row(z, j, c, zl, t), TILE)
                theirs = pl.ds(d_row(z, j, c, 1 - zl, t), TILE)
                pltpu.make_async_copy(w.at[:, mine], wbuf.at[k, zl, :, half], w_l).start()
                push(w.at[:, theirs], wbuf.at[k, zl, :, half], w_s.at[t], w_r.at[t], dev(dzl=1, dzh=t), keep=False)

    def forward(k):
        down, upw = (y + 3) % 4, (y + 1) % 4
        landed(ogb.at[k, slot(down), :], s2_r.at[k, 0])
        part = ogb.at[k, slot(down, 0, 256), :]
        push(part, part, fw_s.at[k, 0], fw_r.at[k, 0], dev(dy=1))
        landed(ogb.at[k, slot(upw), :], s2_r.at[k, 1])
        part = ogb.at[k, slot(upw, 256, 256), :]
        push(part, part, fw_s.at[k, 1], fw_r.at[k, 1], dev(dy=3))

    def grad(k):
        t, j = STEPS[k]
        far = (y + 2) % 4
        landed(ogb.at[k, slot(far, 0, 256), :], fw_r.at[k, 0])
        landed(ogb.at[k, slot(far, 256, 256), :], fw_r.at[k, 1])

        @pl.loop(0, 2)
        def _(b):
            prod = jnp.dot(hid[b], ogb[k], preferred_element_type=F32)
            for z in range(2):
                part = prod[:, z * TILE : (z + 1) * TILE]
                if j:
                    rs_send[t, j - 1, z, b] = part.astype(BF)
                else:
                    own[t, z, b] = part

        if j:
            push(rs_send.at[t, j - 1], rs_recv.at[t, j - 1], rs_s.at[t, j - 1], rs_r.at[t, j - 1], dev(dx=j))

    def x_sum(t):
        for j in (1, 2, 3):
            landed(rs_recv.at[t, j - 1], rs_r.at[t, j - 1])

        def total(z, b):
            out = own[t, z, b]
            for j in range(3):
                out += rs_recv[t, j, z, b].astype(F32)
            return out

        for n, (z, b) in enumerate(((1 - zh, zl), (zh, 1 - zl), (1 - zh, 1 - zl))):
            zs_send[t, n] = total(z, b).astype(BF)
            to = (dev(dzh=1), dev(dzl=1), dev(dzh=1, dzl=1))[n]
            push(zs_send.at[t, n], zs_recv.at[t, n], zs_s.at[t, n], zs_r.at[t, n], to)
        gk[t] = total(zh, zl)

    def block(zh2, x2, c2, t, lo=0, size=HB):
        r = zh2 * 8 + x2 * 2 + c2
        return dirs.at[pl.ds(lo, size), pl.ds(pl.multiple_of(r * ROWS + t * 256, 256), 256)]

    def adam(t):
        for n in range(3):
            landed(zs_recv.at[t, n], zs_r.at[t, n])
        mine = gk[t] + zs_recv[t, 0].astype(F32)
        others = zs_recv[t, 1].astype(F32) + zs_recv[t, 2].astype(F32)
        for half, g_sum in ((zl, mine), (1 - zl, others)):
            g = g_sum * factor
            cols = pl.ds(pl.multiple_of(t * 256 + half * TILE, TILE), TILE)
            first_new = beta_one * m[:, cols] + (1.0 - beta_one) * g
            second_new = beta_two * v[:, cols] + (1.0 - beta_two) * g * g
            first[:, cols] = first_new
            second[:, cols] = second_new
            direction = first_new / bias_one / (jnp.sqrt(second_new / bias_two) + epsilon)
            dir_own[t, :, pl.ds(pl.multiple_of(half * TILE, TILE), TILE)] = direction.astype(BF)
        place, src = block(zh, x, c, t), dir_own.at[t]
        push(src, place, a_s.at[t], a_r.at[t], dev(dzh=1))
        for j in (1, 3):
            push(src, place, b_s.at[t, j, 0], b_r.at[t, j, 0], dev(dx=j))
        push(src, place, c_s.at[t, 0, 0], c_r.at[t, 0, 0], dev(dc=1))
        pltpu.make_async_copy(src, place, a_l.at[t]).start()

    def dir_x(t):
        blk = block(1 - zh, x, c, t)
        landed(blk, a_r.at[t])
        for j in (1, 3):
            push(blk, blk, b_s.at[t, j, 1], b_r.at[t, j, 1], dev(dx=j))
        push(blk, blk, c_s.at[t, 0, 1], c_r.at[t, 0, 1], dev(dc=1))

    def dir_fw(t, n):
        z = zh if n == 0 else 1 - zh
        for j, lo in ((1, 0), (3, HB // 2)):
            blk = block(z, (x - j) % 4, c, t)
            landed(blk, b_r.at[t, j, n])
            part = block(z, (x - j) % 4, c, t, lo, HB // 2)
            push(part, part, f_s.at[t, j, n], f_r.at[t, j, n], dev(dx=j))
            push(blk, blk, c_s.at[t, j, n], c_r.at[t, j, n], dev(dc=1))

    def dir_far(t, n):
        z, far = zh if n == 0 else 1 - zh, (x + 2) % 4
        for j, lo in ((1, 0), (3, HB // 2)):
            landed(block(z, far, c, t, lo, HB // 2), f_r.at[t, j, n])
        blk = block(z, far, c, t)
        push(blk, blk, c_s.at[t, 2, n], c_r.at[t, 2, n], dev(dc=1))

    def dir_end(t):
        landed(block(zh, x, c, t), a_l.at[t])
        for j in range(4):
            for n in range(2):
                landed(block(zh if n == 0 else 1 - zh, (x - j) % 4, 1 - c, t), c_r.at[t, j, n])

    def dh_dots(i, b, ks):
        total = None
        for k in ks:
            part = lax.dot_general(
                wbuf[k, b], ogb[k, slot((y + Y_ORDER[i]) % 4), :],
                (((1,), (1,)), ((), ())), preferred_element_type=F32,
            )
            total = part if total is None else total + part
        return total

    def dh_early(i):
        @pl.loop(0, 2)
        def _(b):
            dk[i, b] = dh_dots(i, b, range(4))

    def lanes(zz):
        return pl.ds(pl.multiple_of(zz * TB, TB), TB)

    def dh_late(i):
        @pl.loop(0, 2)
        def _(b):
            total = dh_dots(i, b, range(4, 8)) + dk[i, b]
            for zz in range(2):
                lo = total[:, zz * 256 : zz * 256 + 128]
                hi = total[:, zz * 256 + 128 : zz * 256 + 256]
                dk[i, b, :, lanes(zz)] = jnp.where(c == 0, lo, hi)
                cs_send[i, zz, b] = jnp.where(c == 0, hi, lo).astype(BF)

        push(cs_send.at[i], cs_recv.at[i], cs_s.at[i], cs_r.at[i], dev(dc=1))

    def dh_core(i):
        landed(cs_recv.at[i], cs_r.at[i])

        @pl.loop(0, 2)
        def _(b):
            dk[i, b, :, lanes(zl)] = dk[i, b, :, lanes(zl)] + cs_recv[i, zl, b].astype(F32)
            zd_send[i, b] = (dk[i, b, :, lanes(1 - zl)] + cs_recv[i, 1 - zl, b].astype(F32)).astype(BF)

        push(zd_send.at[i], zd_recv.at[i], zd_s.at[i], zd_r.at[i], dev(dzl=1))

    def dh_z(i):
        landed(zd_recv.at[i], zd_r.at[i])
        dy = Y_ORDER[i]
        for b in range(2):
            total = (dk[i, b, :, lanes(zl)] + zd_recv[i, b].astype(F32)).astype(BF)
            if dy:
                yd_send[i, b] = total
            else:
                yd_recv[y, b] = total
        if dy:
            push(yd_send.at[i], yd_recv.at[y], yd_s.at[i], yd_r.at[i], dev(dy=dy))

    def cotangents():
        for i in range(3):
            ys = (y - Y_ORDER[i]) % 4
            landed(yd_recv.at[ys], yd_r.at[i])
        for b in range(2):
            for ys in range(4):
                d_own[pl.ds((b * 4 + ys) * HB, HB), :] = yd_recv[ys, b]
        for i in range(28):
            cols = pl.ds(i * 128, 128)
            d = d_own[cols, :].astype(F32).T
            g = gate[:, cols].astype(F32)
            u = up[:, cols].astype(F32)
            sig = jax.nn.sigmoid(g)
            dgu[0, :, cols] = (d * u * sig * (1.0 + g * (1.0 - sig))).astype(BF)
            dgu[1, :, cols] = (d * (g * sig)).astype(BF)

    for n in range(1, 4):
        hid_y(n)
    hid_y(0)
    quarter(0)
    hid_z(0)
    quarter(1)
    spread(0)
    hid_z(1)
    hid_z(2)
    quarter(2)
    spread(1)
    hid_core(0)
    hid_z(3)
    quarter(3)
    quarter(4)
    hid_core(1)
    quarter(5)
    quarter(6)
    quarter(7)
    forward(0)
    spread(2)
    hid_core(2)
    forward(1)
    hid_core(3)
    spread(3)
    for n in range(4):
        hid_end(n)
    grad(0)
    weights()
    forward(2)
    spread(4)
    grad(1)
    forward(3)
    spread(5)
    grad(2)
    forward(4)
    spread(6)
    grad(3)
    x_sum(0)
    forward(5)
    spread(7)
    grad(4)
    adam(0)
    landed(wbuf.at[:, zl], w_l)
    landed(wbuf.at[pl.ds(0, 4), 1 - zl], w_r.at[0])
    dh_early(0)
    forward(6)
    dir_x(0)
    grad(5)
    dh_early(1)
    dh_early(2)
    forward(7)
    grad(6)
    dir_fw(0, 0)
    dh_early(3)
    grad(7)
    landed(wbuf.at[pl.ds(4, 4), 1 - zl], w_r.at[1])
    dh_late(0)
    dh_late(1)
    dh_core(0)
    x_sum(1)
    dir_fw(0, 1)
    dh_late(2)
    dh_late(3)
    dir_far(0, 0)
    adam(1)
    dh_core(1)
    dh_z(0)
    dir_far(0, 1)
    dh_core(2)
    dir_x(1)
    dir_fw(1, 0)
    dh_z(1)
    dh_core(3)
    dir_fw(1, 1)
    dh_z(2)
    dir_far(1, 0)
    dir_far(1, 1)
    dh_z(3)
    cotangents()
    dir_end(0)
    dir_end(1)

    for src, sem in sends:
        landed(src, sem)
    for k in range(8):
        landed(ogb.at[k, pl.ds(0, 384), :], s1_s.at[k])
    for t in range(2):
        landed(wbuf.at[pl.ds(t * 4, 4), 0], w_s.at[t])


def local(gate_pre, up_pre, out_grad, w_down, m_down, v_down):
    vmem = pl.BlockSpec(memory_space=pltpu.VMEM)
    hbm = pl.BlockSpec(memory_space=pl.ANY)
    dma = pltpu.SemaphoreType.DMA
    scratch = [
        pltpu.VMEM((8 * HB, TB), BF),
        pltpu.VMEM((8 * HB, TB), BF),
        pltpu.VMEM((2, HB, 16 * TB), BF),
        pltpu.VMEM((8, 2048, 256), BF),
        pltpu.VMEM((8, 2, HB, 256), BF),
        pltpu.VMEM((2, 3, 2, 2, HB, TILE), BF),
        pltpu.VMEM((2, 3, 2, 2, HB, TILE), BF),
        pltpu.VMEM((2, 2, 2, HB, TILE), F32),
        pltpu.VMEM((2, 3, HB, TILE), BF),
        pltpu.VMEM((2, 3, HB, TILE), BF),
        pltpu.VMEM((2, HB, TILE), F32),
        pltpu.VMEM((2, HB, 256), BF),
        pltpu.VMEM((4, 2, HB, 512), F32),
        pltpu.VMEM((4, 2, 2, HB, TB), BF),
        pltpu.VMEM((4, 2, 2, HB, TB), BF),
        pltpu.VMEM((4, 2, HB, TB), BF),
        pltpu.VMEM((4, 2, HB, TB), BF),
        pltpu.VMEM((3, 2, HB, TB), BF),
        pltpu.VMEM((4, 2, HB, TB), BF),
        dma((8,)), dma((8, 4)),
        dma((8, 2)), dma((8, 2)),
        dma((8, 2)), dma((8, 2)),
        dma((4, 2)), dma((4, 2)),
        dma((4, 2)), dma((4, 2)),
        dma((4,)), dma((4,)),
        dma((2,)), dma((2,)), dma,
        dma((2, 3)), dma((2, 3)),
        dma((2, 3)), dma((2, 3)),
        dma((2,)), dma((2,)), dma((2,)),
        dma((2, 4, 2)), dma((2, 4, 2)),
        dma((2, 4, 2)), dma((2, 4, 2)),
        dma((2, 4, 2)), dma((2, 4, 2)),
        dma((4,)), dma((4,)),
        dma((4,)), dma((4,)),
        dma((3,)), dma((3,)),
    ]
    dgu, dirs, first, second = pl.pallas_call(
        kernel,
        name="step",
        out_shape=(
            jax.ShapeDtypeStruct((2, TB, 8 * HB), BF),
            jax.ShapeDtypeStruct((HB, 16 * ROWS), BF),
            jax.ShapeDtypeStruct((HB, ROWS), F32),
            jax.ShapeDtypeStruct((HB, ROWS), F32),
        ),
        in_specs=[vmem, vmem, vmem, hbm, vmem, vmem],
        out_specs=(vmem, hbm, vmem, vmem),
        scratch_shapes=scratch,
        compiler_params=pltpu.CompilerParams(
            collective_id=0, has_side_effects=True, vmem_limit_bytes=60 << 20
        ),
        cost_estimate=pl.CostEstimate(flops=15 * 10**9, bytes_accessed=40 * 10**6, transcendentals=0),
    )(gate_pre, up_pre, out_grad, w_down.T, m_down.T, v_down.T)
    return (dgu.transpose(1, 0, 2), dirs.T, first.T, second.T)


def solution(mesh):
    return jax.shard_map(
        local,
        mesh=mesh,
        in_specs=(
            P(("replica", "shard"), None),
            P(("replica", "shard"), None),
            P(("replica", "shard"), None),
            P(None, "shard"),
            P("replica", "shard"),
            P("replica", "shard"),
        ),
        out_specs=(
            P(("replica", "shard"), None, None),
            P(None, "shard"),
            P("replica", "shard"),
            P("replica", "shard"),
        ),
        check_vma=False,
    )
```

```python
import math

import jax
import jax.numpy as jnp
from jax import lax
from jax.experimental import pallas as pl
from jax.experimental.pallas import tpu as pltpu
from jax.sharding import PartitionSpec as P

beta_one = 0.9
beta_two = 0.95
epsilon = 1e-08
bias_one = 1.0 - beta_one**10
bias_two = 1.0 - beta_two**10

MESH = pl.DeviceIdType.MESH
BF = jnp.bfloat16
F32 = jnp.float32

TB = 128
HB = 448
ROWS = 512
TILE = 128
PAIRS = (((0, 2), (1, 2)), ((0, 1), (0, 3)), ((1, 1), (1, 3)), ((0, 0), (1, 0)))
Y_ORDER = (2, 1, 3, 0)
STEPS = [(t, pair) for t in range(2) for pair in PAIRS]


def kernel(
    gate, up, og, w, m, v,
    dgu, dirs, first, second,
    hid_own, d_own, hid, ogb, wbuf, rs_send, rs_recv, own, zs_send, zs_recv, gk, dir_own,
    dk, cs_send, cs_recv, zd_send, zd_recv, yd_send, yd_recv,
    s1_s, s1_r, s2_s, s2_r, fw_s, fw_r, h1_s, h1_r, h2_s, h2_r, h3_s, h3_r, w_s, w_r, w_l,
    rs_s, rs_r, zs_s, zs_r, a_l, a_s, a_r, b_s, b_r, f_s, f_r, c_s, c_r,
    cs_s, cs_r, zd_s, zd_r, yd_s, yd_r,
):
    rep, sh = lax.axis_index("replica"), lax.axis_index("shard")
    zh, x, c = rep // 8, (rep // 2) % 4, rep % 2
    zl, y = sh // 4, sh % 4
    q = zl * 2 + c
    factor = 1.0 / math.sqrt(TB * 128)
    sends = []

    def dev(dzh=0, dx=0, dc=0, dzl=0, dy=0):
        return {
            "replica": ((zh + dzh) % 2) * 8 + ((x + dx) % 4) * 2 + (c + dc) % 2,
            "shard": ((zl + dzl) % 2) * 4 + (y + dy) % 4,
        }

    def push(src, dst, ssem, rsem, to, keep=True):
        cp = pltpu.make_async_remote_copy(
            src_ref=src, dst_ref=dst, send_sem=ssem, recv_sem=rsem, device_id=to, device_id_type=MESH
        )
        cp.start()
        if keep:
            sends.append((src, ssem))

    def landed(ref, sem):
        pltpu.make_async_copy(ref, ref, sem).wait()

    for i in range(28):
        cols = pl.ds(i * 128, 128)
        g = gate[:, cols].astype(F32)
        u = up[:, cols].astype(F32)
        hid_own[cols, :] = (g * jax.nn.sigmoid(g) * u).T.astype(BF)

    peers = [dev(dc=1), dev(dzl=1), dev(dzl=1, dc=1), dev(dzh=1), dev(dzh=1, dzl=1)]
    peers += [dev(dy=d) for d in (1, 2, 3)] + [dev(dx=d) for d in (1, 2, 3)]
    barrier = pltpu.get_barrier_semaphore()
    for peer in peers:
        pl.semaphore_signal(barrier, inc=1, device_id=peer, device_id_type=MESH)
    pl.semaphore_wait(barrier, len(peers))

    def tok(yy, qq):
        return pl.ds(pl.multiple_of((yy * 4 + qq) * TB, TB), TB)

    def d_row(zh2, dx, c2, zl2, t):
        r = zh2 * 8 + ((x + dx) % 4) * 2 + c2
        return pl.multiple_of(r * ROWS + t * 256 + zl2 * TILE, TILE)

    def slot(yy, lo=0, n=512):
        return pl.ds(pl.multiple_of(yy * 512 + lo, 128), n)

    H_ORDER = (0, 1, 3, 2)

    def hid_y(n):
        dy = H_ORDER[n]
        for b in range(2):
            rows = pl.ds(pl.multiple_of((b * 4 + (y + dy) % 4) * HB, 16), HB)
            src, dst = hid_own.at[rows, :], hid.at[b, :, tok(y, q)]
            if dy:
                push(src, dst, h1_s.at[n, b], h1_r.at[n, b], dev(dy=dy))
            else:
                pltpu.make_async_copy(src, dst, h1_r.at[n, b]).start()

    def hid_z(n):
        ys = (y - H_ORDER[n]) % 4
        for b in range(2):
            landed(hid.at[b, :, tok(ys, q)], h1_r.at[n, b])
        blk = hid.at[:, :, tok(ys, q)]
        push(blk, blk, h2_s.at[n, 0], h2_r.at[n, 0], dev(dzl=1))
        push(blk, blk, h2_s.at[n, 1], h2_r.at[n, 1], dev(dc=1))

    def hid_core(n):
        ys = (y - H_ORDER[n]) % 4
        blk = hid.at[:, :, tok(ys, (1 - zl) * 2 + c)]
        landed(blk, h2_r.at[n, 0])
        push(blk, blk, h3_s.at[n], h3_r.at[n], dev(dc=1))

    def hid_end(n):
        ys = (y - H_ORDER[n]) % 4
        landed(hid.at[:, :, tok(ys, zl * 2 + 1 - c)], h2_r.at[n, 1])
        landed(hid.at[:, :, tok(ys, (1 - zl) * 2 + 1 - c)], h3_r.at[n])

    def quarter(k):
        t, pair = STEPS[k]
        for dzl, dc in ((1, 0), (1, 1), (0, 1), (0, 0)):
            for p, (z, j) in enumerate(pair):
                cols = pl.ds(d_row(z, j, (c + dc) % 2, (zl + dzl) % 2, t), TILE)
                dst = ogb.at[k, tok(y, q), pl.ds(p * TILE, TILE)]
                if dzl or dc:
                    push(og.at[:, cols], dst, s1_s.at[k], s1_r.at[k, q], dev(dc=dc, dzl=dzl), keep=False)
                else:
                    pltpu.make_async_copy(og.at[:, cols], dst, s1_r.at[k, q]).start()

    def spread(k):
        for qq in range(4):
            landed(ogb.at[k, tok(y, qq), :], s1_r.at[k, qq])
        for n, dy in enumerate((1, 3)):
            push(ogb.at[k, slot(y), :], ogb.at[k, slot(y), :], s2_s.at[k, n], s2_r.at[k, n], dev(dy=dy))

    def weights():
        for k, (t, pair) in enumerate(STEPS):
            for p, (z, j) in enumerate(pair):
                half = pl.ds(p * TILE, TILE)
                mine = pl.ds(d_row(z, j, c, zl, t), TILE)
                theirs = pl.ds(d_row(z, j, c, 1 - zl, t), TILE)
                pltpu.make_async_copy(w.at[:, mine], wbuf.at[k, zl, :, half], w_l).start()
                push(w.at[:, theirs], wbuf.at[k, zl, :, half], w_s.at[t], w_r.at[t], dev(dzl=1, dzh=t), keep=False)

    def forward(k):
        down, upw = (y + 3) % 4, (y + 1) % 4
        landed(ogb.at[k, slot(down), :], s2_r.at[k, 0])
        part = ogb.at[k, slot(down, 0, 256), :]
        push(part, part, fw_s.at[k, 0], fw_r.at[k, 0], dev(dy=1))
        landed(ogb.at[k, slot(upw), :], s2_r.at[k, 1])
        part = ogb.at[k, slot(upw, 256, 256), :]
        push(part, part, fw_s.at[k, 1], fw_r.at[k, 1], dev(dy=3))

    def grad(k):
        t, pair = STEPS[k]
        far = (y + 2) % 4
        landed(ogb.at[k, slot(far, 0, 256), :], fw_r.at[k, 0])
        landed(ogb.at[k, slot(far, 256, 256), :], fw_r.at[k, 1])

        @pl.loop(0, 2)
        def _(b):
            prod = jnp.dot(hid[b], ogb[k], preferred_element_type=F32)
            for p, (z, j) in enumerate(pair):
                part = prod[:, p * TILE : (p + 1) * TILE]
                if j:
                    rs_send[t, j - 1, z, b] = part.astype(BF)
                else:
                    own[t, z, b] = part

        for z, j in pair:
            if j:
                at = (t, j - 1, z)
                push(rs_send.at[at], rs_recv.at[at], rs_s.at[at], rs_r.at[at], dev(dx=j))

    def x_sum(t):
        for j in (1, 2, 3):
            for z in range(2):
                landed(rs_recv.at[t, j - 1, z], rs_r.at[t, j - 1, z])

        def total(z, b):
            out = own[t, z, b]
            for j in range(3):
                out += rs_recv[t, j, z, b].astype(F32)
            return out

        for n, (z, b) in enumerate(((1 - zh, zl), (zh, 1 - zl), (1 - zh, 1 - zl))):
            zs_send[t, n] = total(z, b).astype(BF)
            to = (dev(dzh=1), dev(dzl=1), dev(dzh=1, dzl=1))[n]
            push(zs_send.at[t, n], zs_recv.at[t, n], zs_s.at[t, n], zs_r.at[t, n], to)
        gk[t] = total(zh, zl)

    def block(zh2, x2, c2, t, lo=0, size=HB):
        r = zh2 * 8 + x2 * 2 + c2
        return dirs.at[pl.ds(lo, size), pl.ds(pl.multiple_of(r * ROWS + t * 256, 256), 256)]

    def adam(t):
        for n in range(3):
            landed(zs_recv.at[t, n], zs_r.at[t, n])
        mine = gk[t] + zs_recv[t, 0].astype(F32)
        others = zs_recv[t, 1].astype(F32) + zs_recv[t, 2].astype(F32)
        for half, g_sum in ((zl, mine), (1 - zl, others)):
            g = g_sum * factor
            cols = pl.ds(pl.multiple_of(t * 256 + half * TILE, TILE), TILE)
            first_new = beta_one * m[:, cols] + (1.0 - beta_one) * g
            second_new = beta_two * v[:, cols] + (1.0 - beta_two) * g * g
            first[:, cols] = first_new
            second[:, cols] = second_new
            direction = first_new / bias_one / (jnp.sqrt(second_new / bias_two) + epsilon)
            dir_own[t, :, pl.ds(pl.multiple_of(half * TILE, TILE), TILE)] = direction.astype(BF)
        place, src = block(zh, x, c, t), dir_own.at[t]
        push(src, place, a_s.at[t], a_r.at[t], dev(dzh=1))
        for j in (1, 3):
            push(src, place, b_s.at[t, j, 0], b_r.at[t, j, 0], dev(dx=j))
        push(src, place, c_s.at[t, 0, 0], c_r.at[t, 0, 0], dev(dc=1))
        pltpu.make_async_copy(src, place, a_l.at[t]).start()

    def dir_x(t):
        blk = block(1 - zh, x, c, t)
        landed(blk, a_r.at[t])
        for j in (1, 3):
            push(blk, blk, b_s.at[t, j, 1], b_r.at[t, j, 1], dev(dx=j))
        push(blk, blk, c_s.at[t, 0, 1], c_r.at[t, 0, 1], dev(dc=1))

    def dir_fw(t, n):
        z = zh if n == 0 else 1 - zh
        for j, lo in ((1, 0), (3, HB // 2)):
            blk = block(z, (x - j) % 4, c, t)
            landed(blk, b_r.at[t, j, n])
            part = block(z, (x - j) % 4, c, t, lo, HB // 2)
            push(part, part, f_s.at[t, j, n], f_r.at[t, j, n], dev(dx=j))
            push(blk, blk, c_s.at[t, j, n], c_r.at[t, j, n], dev(dc=1))

    def dir_far(t, n):
        z, far = zh if n == 0 else 1 - zh, (x + 2) % 4
        for j, lo in ((1, 0), (3, HB // 2)):
            landed(block(z, far, c, t, lo, HB // 2), f_r.at[t, j, n])
        blk = block(z, far, c, t)
        push(blk, blk, c_s.at[t, 2, n], c_r.at[t, 2, n], dev(dc=1))

    def dir_end(t):
        landed(block(zh, x, c, t), a_l.at[t])
        for j in range(4):
            for n in range(2):
                landed(block(zh if n == 0 else 1 - zh, (x - j) % 4, 1 - c, t), c_r.at[t, j, n])

    def dh_dots(i, b, ks):
        total = None
        for k in ks:
            part = lax.dot_general(
                wbuf[k, b], ogb[k, slot((y + Y_ORDER[i]) % 4), :],
                (((1,), (1,)), ((), ())), preferred_element_type=F32,
            )
            total = part if total is None else total + part
        return total

    def dh_early(i):
        @pl.loop(0, 2)
        def _(b):
            dk[i, b] = dh_dots(i, b, range(4))

    def lanes(zz):
        return pl.ds(pl.multiple_of(zz * TB, TB), TB)

    def dh_late(i):
        @pl.loop(0, 2)
        def _(b):
            total = dh_dots(i, b, range(4, 8)) + dk[i, b]
            for zz in range(2):
                lo = total[:, zz * 256 : zz * 256 + 128]
                hi = total[:, zz * 256 + 128 : zz * 256 + 256]
                dk[i, b, :, lanes(zz)] = jnp.where(c == 0, lo, hi)
                cs_send[i, zz, b] = jnp.where(c == 0, hi, lo).astype(BF)

        push(cs_send.at[i], cs_recv.at[i], cs_s.at[i], cs_r.at[i], dev(dc=1))

    def dh_core(i):
        landed(cs_recv.at[i], cs_r.at[i])

        @pl.loop(0, 2)
        def _(b):
            dk[i, b, :, lanes(zl)] = dk[i, b, :, lanes(zl)] + cs_recv[i, zl, b].astype(F32)
            zd_send[i, b] = (dk[i, b, :, lanes(1 - zl)] + cs_recv[i, 1 - zl, b].astype(F32)).astype(BF)

        push(zd_send.at[i], zd_recv.at[i], zd_s.at[i], zd_r.at[i], dev(dzl=1))

    def dh_z(i):
        landed(zd_recv.at[i], zd_r.at[i])
        dy = Y_ORDER[i]
        for b in range(2):
            total = (dk[i, b, :, lanes(zl)] + zd_recv[i, b].astype(F32)).astype(BF)
            if dy:
                yd_send[i, b] = total
            else:
                yd_recv[y, b] = total
        if dy:
            push(yd_send.at[i], yd_recv.at[y], yd_s.at[i], yd_r.at[i], dev(dy=dy))

    def cotangents():
        for i in range(3):
            ys = (y - Y_ORDER[i]) % 4
            landed(yd_recv.at[ys], yd_r.at[i])
        for b in range(2):
            for ys in range(4):
                d_own[pl.ds((b * 4 + ys) * HB, HB), :] = yd_recv[ys, b]
        for i in range(28):
            cols = pl.ds(i * 128, 128)
            d = d_own[cols, :].astype(F32).T
            g = gate[:, cols].astype(F32)
            u = up[:, cols].astype(F32)
            sig = jax.nn.sigmoid(g)
            dgu[0, :, cols] = (d * u * sig * (1.0 + g * (1.0 - sig))).astype(BF)
            dgu[1, :, cols] = (d * (g * sig)).astype(BF)

    for n in range(1, 4):
        hid_y(n)
    hid_y(0)
    quarter(0)
    hid_z(0)
    quarter(1)
    spread(0)
    hid_z(1)
    hid_z(2)
    quarter(2)
    spread(1)
    hid_core(0)
    hid_z(3)
    quarter(3)
    quarter(4)
    hid_core(1)
    quarter(5)
    quarter(6)
    quarter(7)
    forward(0)
    spread(2)
    hid_core(2)
    forward(1)
    hid_core(3)
    spread(3)
    for n in range(4):
        hid_end(n)
    grad(0)
    weights()
    forward(2)
    spread(4)
    grad(1)
    forward(3)
    spread(5)
    grad(2)
    forward(4)
    spread(6)
    grad(3)
    x_sum(0)
    forward(5)
    spread(7)
    grad(4)
    adam(0)
    landed(wbuf.at[:, zl], w_l)
    landed(wbuf.at[pl.ds(0, 4), 1 - zl], w_r.at[0])
    dh_early(0)
    forward(6)
    dir_x(0)
    grad(5)
    dh_early(1)
    dh_early(2)
    forward(7)
    grad(6)
    dir_fw(0, 0)
    dh_early(3)
    grad(7)
    landed(wbuf.at[pl.ds(4, 4), 1 - zl], w_r.at[1])
    dh_late(0)
    dh_late(1)
    dh_core(0)
    x_sum(1)
    dir_fw(0, 1)
    dh_late(2)
    dh_late(3)
    dir_far(0, 0)
    adam(1)
    dh_core(1)
    dh_z(0)
    dir_far(0, 1)
    dh_core(2)
    dir_x(1)
    dir_fw(1, 0)
    dh_z(1)
    dh_core(3)
    dir_fw(1, 1)
    dh_z(2)
    dir_far(1, 0)
    dir_far(1, 1)
    dh_z(3)
    cotangents()
    dir_end(0)
    dir_end(1)

    for src, sem in sends:
        landed(src, sem)
    for k in range(8):
        landed(ogb.at[k, pl.ds(0, 384), :], s1_s.at[k])
    for t in range(2):
        landed(wbuf.at[pl.ds(t * 4, 4), 0], w_s.at[t])


def local(gate_pre, up_pre, out_grad, w_down, m_down, v_down):
    vmem = pl.BlockSpec(memory_space=pltpu.VMEM)
    hbm = pl.BlockSpec(memory_space=pl.ANY)
    dma = pltpu.SemaphoreType.DMA
    scratch = [
        pltpu.VMEM((8 * HB, TB), BF),
        pltpu.VMEM((8 * HB, TB), BF),
        pltpu.VMEM((2, HB, 16 * TB), BF),
        pltpu.VMEM((8, 2048, 256), BF),
        pltpu.VMEM((8, 2, HB, 256), BF),
        pltpu.VMEM((2, 3, 2, 2, HB, TILE), BF),
        pltpu.VMEM((2, 3, 2, 2, HB, TILE), BF),
        pltpu.VMEM((2, 2, 2, HB, TILE), F32),
        pltpu.VMEM((2, 3, HB, TILE), BF),
        pltpu.VMEM((2, 3, HB, TILE), BF),
        pltpu.VMEM((2, HB, TILE), F32),
        pltpu.VMEM((2, HB, 256), BF),
        pltpu.VMEM((4, 2, HB, 512), F32),
        pltpu.VMEM((4, 2, 2, HB, TB), BF),
        pltpu.VMEM((4, 2, 2, HB, TB), BF),
        pltpu.VMEM((4, 2, HB, TB), BF),
        pltpu.VMEM((4, 2, HB, TB), BF),
        pltpu.VMEM((3, 2, HB, TB), BF),
        pltpu.VMEM((4, 2, HB, TB), BF),
        dma((8,)), dma((8, 4)),
        dma((8, 2)), dma((8, 2)),
        dma((8, 2)), dma((8, 2)),
        dma((4, 2)), dma((4, 2)),
        dma((4, 2)), dma((4, 2)),
        dma((4,)), dma((4,)),
        dma((2,)), dma((2,)), dma,
        dma((2, 3, 2)), dma((2, 3, 2)),
        dma((2, 3)), dma((2, 3)),
        dma((2,)), dma((2,)), dma((2,)),
        dma((2, 4, 2)), dma((2, 4, 2)),
        dma((2, 4, 2)), dma((2, 4, 2)),
        dma((2, 4, 2)), dma((2, 4, 2)),
        dma((4,)), dma((4,)),
        dma((4,)), dma((4,)),
        dma((3,)), dma((3,)),
    ]
    dgu, dirs, first, second = pl.pallas_call(
        kernel,
        name="step",
        out_shape=(
            jax.ShapeDtypeStruct((2, TB, 8 * HB), BF),
            jax.ShapeDtypeStruct((HB, 16 * ROWS), BF),
            jax.ShapeDtypeStruct((HB, ROWS), F32),
            jax.ShapeDtypeStruct((HB, ROWS), F32),
        ),
        in_specs=[vmem, vmem, vmem, hbm, vmem, vmem],
        out_specs=(vmem, hbm, vmem, vmem),
        scratch_shapes=scratch,
        compiler_params=pltpu.CompilerParams(
            collective_id=0, has_side_effects=True, vmem_limit_bytes=60 << 20
        ),
        cost_estimate=pl.CostEstimate(flops=15 * 10**9, bytes_accessed=40 * 10**6, transcendentals=0),
    )(gate_pre, up_pre, out_grad, w_down.T, m_down.T, v_down.T)
    return (dgu.transpose(1, 0, 2), dirs.T, first.T, second.T)


def solution(mesh):
    return jax.shard_map(
        local,
        mesh=mesh,
        in_specs=(
            P(("replica", "shard"), None),
            P(("replica", "shard"), None),
            P(("replica", "shard"), None),
            P(None, "shard"),
            P("replica", "shard"),
            P("replica", "shard"),
        ),
        out_specs=(
            P(("replica", "shard"), None, None),
            P(None, "shard"),
            P("replica", "shard"),
            P("replica", "shard"),
        ),
        check_vma=False,
    )
```
